32 devices in a mesh: obs: 4 (over x, core), par: 8 (over z, y).
Axes of the slice: x: 2, y: 2, z: 4, core: 2. Of those that a mesh axis runs over, the one named last changes fastest.
Arguments:
- jacobian: bfloat16 [768, 16384], P(('obs', 'par')), may hold values from -0.21875 to 0.21875
- obs_weights: float32 [768], replicated, may hold values from 0.1 to 10
- time_to_obs: int32 [768], P(('obs', 'par')), may hold values from 0 to 767, each once
Outputs:
- normal_matrix: float32 [16384, 16384], P('obs', 'par')
The draws below stay inside these ranges and needn't reach their ends.
Inputs may be any that keep to these rules, and one draw needn't show every extreme that they name: `time_to_obs`: each observation index appears exactly once.
All inputs are finite; a program needn't handle non-finite values.
Results may differ from the reference program's by a relative error of at most 0.0039.
Values may be sent and summed in bfloat16 or wider, within the bound.
A program may use at most 128 MiB of HBM per device.

```python
import math
import jax
import jax.numpy as jnp

PARAMS = 16384
ROWS = 768


def block_scale(own_key, dims, split, low, top_value):
    level, own = 1.0, jax.random.fold_in(own_key, 6)
    for position, shards_of in split:
        steps = jnp.exp(jax.random.uniform(jax.random.fold_in(own, position), (shards_of,), jnp.float32, low / len(split), top_value / len(split)))
        level = level * jnp.repeat(steps, dims[position] // shards_of).reshape([-1 if axis == position else 1 for axis in range(len(dims))])
    return level


def centred(rng, dims, spread, bound, cuts=(), dtype=jnp.bfloat16):
    result = jax.random.normal(rng, dims, jnp.float32) * spread
    if len(cuts) > 0:
        result = block_scale(rng, dims, cuts, -0.22, 0.18) * result
    return jnp.clip(result, min=-bound, max=bound).astype(dtype)


def setup_inputs(seed: int = 0) -> dict:
    arg_keys = jax.random.split(jax.random.key(seed), 4)
    return {
        "jacobian": centred(arg_keys[0], (ROWS, PARAMS), ROWS ** -0.5, 0.21875, ((0, 32),)),
        "obs_weights": jnp.clip(jnp.exp(jax.random.uniform(arg_keys[1], (ROWS,), jnp.float32, math.log(0.1), math.log(10.0))), 0.1, 10.0),
        "time_to_obs": jax.random.permutation(arg_keys[2], ROWS).astype(jnp.int32),
    }


def reference(jacobian, obs_weights, time_to_obs):
    row_weight = obs_weights[time_to_obs]
    scaled = (jnp.sqrt(row_weight)[:, None] * jacobian.astype(jnp.float32)).astype(jnp.bfloat16)
    return jnp.dot(scaled.T, scaled, preferred_element_type=jnp.float32)
```

```python
import functools
import itertools

import jax
import jax.numpy as jnp
from jax import lax
from jax.experimental import pallas as pl
from jax.experimental.pallas import tpu as pltpu
from jax.sharding import PartitionSpec as P

MESH = pl.DeviceIdType.MESH
LAG = 12


def grid_of(par_count):
    return {8: (4, 2), 32: (4, 4, 2)}.get(par_count, (par_count,))


def schedule(dims):
    spans = [(0, 1) if n == 2 else tuple(range(1 - n, n)) for n in dims]
    steps = [(off, turn) for off in itertools.product(*spans) for turn in range(4)]
    late = (0.0, 0.0, 0.5, 0.5)
    return sorted(
        steps,
        key=lambda s: (sum(abs(o) for o in s[0]) + late[s[1]], s[1], [abs(o) for o in reversed(s[0])], s[0]),
    )


def guarded(conds, action):
    if not conds:
        action()
        return
    both = conds[0]
    for cond in conds[1:]:
        both = jnp.logical_and(both, cond)
    pl.when(both)(action)


def gather_kernel(dims, late_first, scaled, panel, cols, own_sem, recv, col_recv, obs_send, par_send, col_send):
    a, b = lax.axis_index("obs"), lax.axis_index("par")
    core, chip = a % 2, a // 2
    quarter, width = panel.shape[2], cols.shape[2]
    per = quarter // width
    is_owner = a == b // per
    on_owner_chip = chip == (b // per) // 2
    strides, where = [], []
    stride = 1
    for n in reversed(dims):
        strides.insert(0, stride)
        where.insert(0, (b // stride) % n)
        stride *= n
    rank = len(dims)

    def obs_of(turn):
        return 2 * ((chip + turn // 2) % 2) + (core + turn % 2) % 2

    def hop(dim, sign):
        n, at = dims[dim], where[dim]
        if n == 2:
            return b + (1 - 2 * at) * strides[dim], []
        return b + sign * strides[dim], [at < n - 1 if sign > 0 else at > 0]

    def remote(src, dst, send_sem, recv_sem, obs, par):
        return pltpu.make_async_remote_copy(
            src_ref=src, dst_ref=dst, send_sem=send_sem, recv_sem=recv_sem,
            device_id=(obs, par), device_id_type=MESH,
        )

    def here(step):
        conds = []
        for dim, off in enumerate(step[0]):
            if dims[dim] > 2 and off:
                conds.append(where[dim] + off < dims[dim] if off > 0 else where[dim] + off >= 0)
        return conds

    def slot_of(step):
        origin = b
        for dim, off in enumerate(step[0]):
            if off:
                origin = origin + ((1 - 2 * where[dim]) if dims[dim] == 2 else off) * strides[dim]
        source = obs_of(step[1])
        return 4 * origin + source, source

    def is_own(step):
        return step[1] == 0 and not any(step[0])

    def view(step, slot):
        if is_own(step):
            return scaled.at[:, pl.ds(pl.multiple_of(a * quarter, 128), quarter)]
        return panel.at[slot]

    def col_view(step, slot):
        if is_own(step):
            return scaled.at[:, pl.ds(pl.multiple_of(b * width, 128), width)]
        return panel.at[slot, :, pl.ds(pl.multiple_of((b % per) * width, 128), width)]

    def forwards(step):
        order = list(range(rank))
        if step[1] == 3 and late_first:
            order = order[::-1]
        moved = [i for i in range(rank) if step[0][order[i]]]
        last = moved[-1] if moved else -1
        out = []
        for i in range(max(last, 0), rank):
            dim = order[i]
            if i == last:
                if dims[dim] > 2:
                    out.append((dim, -1 if step[0][dim] > 0 else 1))
            elif dims[dim] == 2:
                out.append((dim, 1))
            else:
                out += [(dim, 1), (dim, -1)]
        return out

    def par_copy(step, slot, dim, sign):
        return remote(
            view(step, slot), panel.at[slot], par_send.at[2 * dim + (sign > 0), slot], recv.at[slot],
            a, hop(dim, sign)[0],
        )

    def col_copies(step, slot, source):
        src = col_view(step, slot)
        return (
            remote(src, cols.at[slot], col_send.at[0, slot], col_recv.at[slot], 2 * chip + 1 - core, b),
            remote(src, cols.at[slot], col_send.at[1, slot], col_recv.at[slot], 2 * (1 - chip) + source % 2, b),
        )

    def relay(slot):
        return remote(
            cols.at[slot], cols.at[slot], col_send.at[2, slot], col_recv.at[slot], 2 * chip + 1 - core, b
        )

    def arrive(step):
        def run():
            slot, source = slot_of(step)
            if not is_own(step):
                pltpu.make_async_copy(panel.at[slot], panel.at[slot], recv.at[slot]).wait()
            for dim, sign in forwards(step):
                guarded(hop(dim, sign)[1], lambda: par_copy(step, slot, dim, sign).start())

            @pl.when(is_owner)
            def _():
                for copy in col_copies(step, slot, source):
                    copy.start()
                pltpu.make_async_copy(col_view(step, slot), cols.at[slot], col_recv.at[slot]).start()

        guarded(here(step), run)

    def take_cols(step):
        def run():
            slot, source = slot_of(step)
            pltpu.make_async_copy(cols.at[slot], cols.at[slot], col_recv.at[slot]).wait()
            pl.when(jnp.logical_and(jnp.logical_not(on_owner_chip), core == source % 2))(
                lambda: relay(slot).start()
            )

        guarded(here(step), run)

    def finish(step):
        def run():
            slot, source = slot_of(step)
            for dim, sign in forwards(step):
                guarded(hop(dim, sign)[1], lambda: par_copy(step, slot, dim, sign).wait_send())

            @pl.when(is_owner)
            def _():
                for copy in col_copies(step, slot, source):
                    copy.wait_send()

            pl.when(jnp.logical_and(jnp.logical_not(on_owner_chip), core == source % 2))(
                lambda: relay(slot).wait_send()
            )

        guarded(here(step), run)

    barrier = pltpu.get_barrier_semaphore()
    mates = [(obs_of(turn), b, []) for turn in (1, 2, 3)]
    for dim in range(rank):
        for sign in (1,) if dims[dim] == 2 else (1, -1):
            mates.append((a, *hop(dim, sign)))
    for obs, par, conds in mates:
        guarded(conds, lambda: pl.semaphore_signal(barrier, inc=1, device_id=(obs, par), device_id_type=MESH))
    count = sum(not conds for _, _, conds in mates)
    for _, _, conds in mates:
        for cond in conds:
            count = count + cond.astype(jnp.int32)
    pl.semaphore_wait(barrier, count)

    mine = 4 * b + a
    to_obs = []
    for turn in (2, 3, 1):
        obs = obs_of(turn)
        to_obs.append(remote(
            scaled.at[:, pl.ds(pl.multiple_of(obs * quarter, 128), quarter)], panel.at[mine],
            obs_send.at[turn], recv.at[mine], obs, b,
        ))
        to_obs[-1].start()
    keep = pltpu.make_async_copy(
        scaled.at[:, pl.ds(pl.multiple_of(a * quarter, 128), quarter)], panel.at[mine], own_sem.at[0]
    )
    keep.start()
    steps = schedule(dims)
    for i, step in enumerate(steps):
        arrive(step)
        if i >= LAG:
            take_cols(steps[i - LAG])
    for step in steps[-LAG:]:
        take_cols(step)
    keep.wait()
    for copy in to_obs:
        copy.wait_send()
    for step in steps:
        finish(step)


def on_device(obs_count, par_count, jacobian, obs_weights, time_to_obs):
    rows_here, param_count = jacobian.shape
    indices = jnp.arange(obs_weights.shape[0], dtype=jnp.int32)
    picked = jnp.sum(
        jnp.where(time_to_obs[:, None] == indices[None, :], obs_weights[None, :], 0.0), axis=1
    )
    scaled = (jnp.sqrt(picked)[:, None] * jacobian.astype(jnp.float32)).astype(jnp.bfloat16)
    dims = grid_of(par_count)
    slots = obs_count * par_count
    quarter, width = param_count // obs_count, param_count // par_count
    dma = pltpu.SemaphoreType.DMA
    panel, cols = pl.pallas_call(
        functools.partial(gather_kernel, dims, dims == (4, 2)),
        out_shape=(
            jax.ShapeDtypeStruct((slots, rows_here, quarter), jnp.bfloat16),
            jax.ShapeDtypeStruct((slots, rows_here, width), jnp.bfloat16),
        ),
        in_specs=[pl.BlockSpec(memory_space=pl.ANY)],
        out_specs=(pl.BlockSpec(memory_space=pl.ANY),) * 2,
        scratch_shapes=[
            dma((1,)), dma((slots,)), dma((slots,)), dma((4,)), dma((2 * len(dims), slots)), dma((3, slots)),
        ],
        compiler_params=pltpu.CompilerParams(collective_id=0, has_side_effects=True),
        name="gather",
    )(scaled)
    return jnp.einsum("src,srd->cd", panel, cols, preferred_element_type=jnp.float32)


def solution(mesh):
    placed = (P(("obs", "par"), None), P(), P(("obs", "par")))
    return jax.shard_map(
        functools.partial(on_device, mesh.shape["obs"], mesh.shape["par"]),
        mesh=mesh, in_specs=placed, out_specs=P("obs", "par"), check_vma=False,
    )
```

```python
import functools
import itertools

import jax
import jax.numpy as jnp
from jax import lax
from jax.experimental import pallas as pl
from jax.experimental.pallas import tpu as pltpu
from jax.sharding import PartitionSpec as P

MESH = pl.DeviceIdType.MESH
LAG = 12


def grid_of(par_count):
    return {8: (4, 2), 32: (4, 4, 2)}.get(par_count, (par_count,))


def forwards(dims, late_first, step):
    rank = len(dims)
    order = list(range(rank))
    if step[1] == 3 and late_first:
        order = order[::-1]
    moved = [i for i in range(rank) if step[0][order[i]]]
    last = moved[-1] if moved else -1
    out = []
    for i in range(max(last, 0), rank):
        dim = order[i]
        if i == last:
            if dims[dim] > 2:
                out.append((dim, -1 if step[0][dim] > 0 else 1))
        elif dims[dim] == 2:
            out.append((dim, 1))
        else:
            out += [(dim, 1), (dim, -1)]
    return out


def schedule(dims, late_first):
    spans = [(0, 1) if n == 2 else tuple(range(1 - n, n)) for n in dims]
    steps = [(off, turn) for off in itertools.product(*spans) for turn in range(4)]

    def due(step):
        off, turn = step
        away = sum(abs(o) for o in off) + 0.5 * (turn // 2)
        away += 0.75 * (off[-1] != 0)
        return away, turn, [abs(o) for o in reversed(off)], off

    return sorted(steps, key=due)


def sends_at(dims, late_first, place):
    sent = {}
    for step in schedule(dims, late_first):
        if all(0 <= place[dim] + step[0][dim] < dims[dim] for dim in place):
            for dim, sign in forwards(dims, late_first, step):
                if dim not in place or 0 <= place[dim] + sign < dims[dim]:
                    way = 2 * dim + (sign > 0)
                    sent[way] = sent.get(way, 0) + 1
    return sent


def guarded(conds, action):
    if not conds:
        action()
        return
    both = conds[0]
    for cond in conds[1:]:
        both = jnp.logical_and(both, cond)
    pl.when(both)(action)


def gather_kernel(dims, late_first, scaled, panel, cols, own_sem, recv, col_recv, obs_send, par_send, col_send):
    a, b = lax.axis_index("obs"), lax.axis_index("par")
    core, chip = a % 2, a // 2
    quarter, width = panel.shape[2], cols.shape[2]
    per = quarter // width
    is_owner = a == b // per
    on_owner_chip = chip == (b // per) // 2
    strides, where = [], []
    stride = 1
    for n in reversed(dims):
        strides.insert(0, stride)
        where.insert(0, (b // stride) % n)
        stride *= n
    rank = len(dims)

    def obs_of(turn):
        return 2 * ((chip + turn // 2) % 2) + (core + turn % 2) % 2

    def hop(dim, sign):
        n, at = dims[dim], where[dim]
        if n == 2:
            return b + (1 - 2 * at) * strides[dim], []
        return b + sign * strides[dim], [at < n - 1 if sign > 0 else at > 0]

    def remote(src, dst, send_sem, recv_sem, obs, par):
        return pltpu.make_async_remote_copy(
            src_ref=src, dst_ref=dst, send_sem=send_sem, recv_sem=recv_sem,
            device_id=(obs, par), device_id_type=MESH,
        )

    def here(step):
        conds = []
        for dim, off in enumerate(step[0]):
            if dims[dim] > 2 and off:
                conds.append(where[dim] + off < dims[dim] if off > 0 else where[dim] + off >= 0)
        return conds

    def slot_of(step):
        origin = b
        for dim, off in enumerate(step[0]):
            if off:
                origin = origin + ((1 - 2 * where[dim]) if dims[dim] == 2 else off) * strides[dim]
        source = obs_of(step[1])
        return 4 * origin + source, source

    def is_own(step):
        return step[1] == 0 and not any(step[0])

    def view(step, slot):
        if is_own(step):
            return scaled.at[:, pl.ds(pl.multiple_of(a * quarter, 128), quarter)]
        return panel.at[slot]

    def col_view(step, slot):
        if is_own(step):
            return scaled.at[:, pl.ds(pl.multiple_of(b * width, 128), width)]
        return panel.at[slot, :, pl.ds(pl.multiple_of((b % per) * width, 128), width)]

    def par_copy(step, slot, dim, sign):
        return remote(
            view(step, slot), panel.at[slot], par_send.at[2 * dim + (sign > 0)], recv.at[slot],
            a, hop(dim, sign)[0],
        )

    def col_copies(step, slot, source):
        src = col_view(step, slot)
        return (
            remote(src, cols.at[slot], col_send.at[0], col_recv.at[slot], 2 * chip + 1 - core, b),
            remote(src, cols.at[slot], col_send.at[1], col_recv.at[slot], 2 * (1 - chip) + source % 2, b),
        )

    def relay(slot):
        return remote(
            cols.at[slot], cols.at[slot], col_send.at[2], col_recv.at[slot], 2 * chip + 1 - core, b
        )

    def drain(ref, sem):
        pltpu.make_async_copy(ref, ref, sem).wait()

    def arrive(step):
        def run():
            slot, source = slot_of(step)
            if not is_own(step):
                drain(panel.at[slot], recv.at[slot])
            for dim, sign in forwards(dims, late_first, step):
                guarded(hop(dim, sign)[1], lambda: par_copy(step, slot, dim, sign).start())

            @pl.when(is_owner)
            def _():
                for copy in col_copies(step, slot, source):
                    copy.start()

        guarded(here(step), run)

    def take_cols(step):
        def run():
            slot, source = slot_of(step)
            drain(cols.at[slot], col_recv.at[slot])
            pl.when(jnp.logical_and(jnp.logical_not(on_owner_chip), core == source % 2))(
                lambda: relay(slot).start()
            )

        guarded([jnp.logical_not(is_owner), *here(step)], run)

    def finish():
        long = [dim for dim in range(rank) if dims[dim] > 2]
        for place in itertools.product(*(range(dims[dim]) for dim in long)):
            sent = sends_at(dims, late_first, dict(zip(long, place)))

            def run():
                for way in sorted(sent):
                    drain(panel.at[pl.ds(0, sent[way])], par_send.at[way])

            guarded([where[dim] == at for dim, at in zip(long, place)], run)

        @pl.when(is_owner)
        def _():
            drain(cols, col_send.at[0])
            drain(cols, col_send.at[1])

        pl.when(jnp.logical_not(on_owner_chip))(
            lambda: drain(cols.at[pl.ds(0, cols.shape[0] // 2)], col_send.at[2])
        )

    barrier = pltpu.get_barrier_semaphore()
    mates = [(obs_of(turn), b, []) for turn in (1, 2, 3)]
    for dim in range(rank):
        for sign in (1,) if dims[dim] == 2 else (1, -1):
            mates.append((a, *hop(dim, sign)))
    for obs, par, conds in mates:
        guarded(conds, lambda: pl.semaphore_signal(barrier, inc=1, device_id=(obs, par), device_id_type=MESH))
    count = sum(not conds for _, _, conds in mates)
    for _, _, conds in mates:
        for cond in conds:
            count = count + cond.astype(jnp.int32)
    pl.semaphore_wait(barrier, count)

    mine = 4 * b + a
    to_obs = []
    for turn in (2, 3, 1):
        obs = obs_of(turn)
        to_obs.append(remote(
            scaled.at[:, pl.ds(pl.multiple_of(obs * quarter, 128), quarter)], panel.at[mine],
            obs_send.at[turn], recv.at[mine], obs, b,
        ))
        to_obs[-1].start()
    keep = pltpu.make_async_copy(
        scaled.at[:, pl.ds(pl.multiple_of(a * quarter, 128), quarter)], panel.at[mine], own_sem.at[0]
    )
    keep.start()
    steps = schedule(dims, late_first)
    lag = LAG if rank < 3 else len(steps)
    for i, step in enumerate(steps):
        arrive(step)
        if i >= lag:
            take_cols(steps[i - lag])
    for step in steps[-lag:]:
        take_cols(step)
    keep.wait()
    for copy in to_obs:
        copy.wait_send()
    finish()


def product_kernel(per, panel, panel_all, cols, out, right, sem):
    a, b = lax.axis_index("obs"), lax.axis_index("par")
    width = right.shape[1]

    @pl.when(pl.program_id(0) == 0)
    def _():
        own = pl.ds(pl.multiple_of((b % per) * width, 128), width)

        @pl.when(a == b // per)
        def _():
            pltpu.make_async_copy(panel_all.at[:, own], right, sem).start()

        @pl.when(a != b // per)
        def _():
            pltpu.make_async_copy(cols, right, sem).start()

        pltpu.make_async_copy(cols, right, sem).wait()

    out[...] = lax.dot_general(
        panel[...], right[...], (((0,), (0,)), ((), ())), preferred_element_type=jnp.float32
    )


def on_device(obs_count, par_count, jacobian, obs_weights, time_to_obs):
    rows_here, param_count = jacobian.shape
    indices = jnp.arange(obs_weights.shape[0], dtype=jnp.int32)
    picked = jnp.sum(
        jnp.where(time_to_obs[:, None] == indices[None, :], obs_weights[None, :], 0.0), axis=1
    )
    scaled = (jnp.sqrt(picked)[:, None] * jacobian.astype(jnp.float32)).astype(jnp.bfloat16)
    dims = grid_of(par_count)
    slots = obs_count * par_count
    quarter, width = param_count // obs_count, param_count // par_count
    dma = pltpu.SemaphoreType.DMA
    panel, cols = pl.pallas_call(
        functools.partial(gather_kernel, dims, dims == (4, 2)),
        out_shape=(
            jax.ShapeDtypeStruct((slots, rows_here, quarter), jnp.bfloat16),
            jax.ShapeDtypeStruct((slots, rows_here, width), jnp.bfloat16),
        ),
        in_specs=[pl.BlockSpec(memory_space=pl.ANY)],
        out_specs=(pl.BlockSpec(memory_space=pl.ANY),) * 2,
        scratch_shapes=[
            dma((1,)), dma((slots,)), dma((slots,)), dma((4,)), dma((2 * len(dims),)), dma((3,)),
        ],
        compiler_params=pltpu.CompilerParams(collective_id=0, has_side_effects=True),
        name="gather",
    )(scaled)
    rows = slots * rows_here
    panel, cols = panel.reshape(rows, quarter), cols.reshape(rows, width)
    tile = 256
    return pl.pallas_call(
        functools.partial(product_kernel, quarter // width),
        out_shape=jax.ShapeDtypeStruct((quarter, width), jnp.float32),
        grid=(quarter // tile,),
        in_specs=[
            pl.BlockSpec((rows, tile), lambda i: (0, i)),
            pl.BlockSpec(memory_space=pl.ANY),
            pl.BlockSpec(memory_space=pl.ANY),
        ],
        out_specs=pl.BlockSpec((tile, width), lambda i: (i, 0)),
        scratch_shapes=[pltpu.VMEM((rows, width), jnp.bfloat16), dma],
        compiler_params=pltpu.CompilerParams(vmem_limit_bytes=48 * 2**20),
        name="product",
    )(panel, panel, cols)


def solution(mesh):
    placed = (P(("obs", "par"), None), P(), P(("obs", "par")))
    return jax.shard_map(
        functools.partial(on_device, mesh.shape["obs"], mesh.shape["par"]),
        mesh=mesh, in_specs=placed, out_specs=P("obs", "par"), check_vma=False,
    )
```

```python
import functools
import itertools

import jax
import jax.numpy as jnp
from jax import lax
from jax.experimental import pallas as pl
from jax.experimental.pallas import tpu as pltpu
from jax.sharding import PartitionSpec as P

MESH = pl.DeviceIdType.MESH
LAG = 12


def grid_of(par_count):
    return {8: (4, 2), 32: (4, 4, 2)}.get(par_count, (par_count,))


def forwards(dims, late_first, step):
    rank = len(dims)
    order = list(range(rank))
    if step[1] == 3 and late_first:
        order = order[::-1]
    moved = [i for i in range(rank) if step[0][order[i]]]
    last = moved[-1] if moved else -1
    out = []
    for i in range(max(last, 0), rank):
        dim = order[i]
        if i == last:
            if dims[dim] > 2:
                out.append((dim, -1 if step[0][dim] > 0 else 1))
        elif dims[dim] == 2:
            out.append((dim, 1))
        else:
            out += [(dim, 1), (dim, -1)]
    return out


def schedule(dims, late_first):
    spans = [(0, 1) if n == 2 else tuple(range(1 - n, n)) for n in dims]
    steps = [(off, turn) for off in itertools.product(*spans) for turn in range(4)]

    def due(step):
        off, turn = step
        away = sum(abs(o) for o in off) + 0.5 * (turn // 2)
        away += 0.75 * (off[-1] != 0)
        return away, turn, [abs(o) for o in reversed(off)], off

    return sorted(steps, key=due)


def sends_at(dims, late_first, place):
    sent = {}
    for step in schedule(dims, late_first):
        if all(0 <= place[dim] + step[0][dim] < dims[dim] for dim in place):
            for dim, sign in forwards(dims, late_first, step):
                if dim not in place or 0 <= place[dim] + sign < dims[dim]:
                    way = 2 * dim + (sign > 0)
                    sent[way] = sent.get(way, 0) + 1
    return sent


def guarded(conds, action):
    if not conds:
        action()
        return
    both = conds[0]
    for cond in conds[1:]:
        both = jnp.logical_and(both, cond)
    pl.when(both)(action)


def gather_kernel(dims, late_first, scaled, panel, cols, own_sem, recv, col_recv, obs_send, par_send, col_send):
    a, b = lax.axis_index("obs"), lax.axis_index("par")
    core, chip = a % 2, a // 2
    quarter, width = panel.shape[2], cols.shape[2]
    per = quarter // width
    is_owner = a == b // per
    on_owner_chip = chip == (b // per) // 2
    strides, where = [], []
    stride = 1
    for n in reversed(dims):
        strides.insert(0, stride)
        where.insert(0, (b // stride) % n)
        stride *= n
    rank = len(dims)

    def obs_of(turn):
        return 2 * ((chip + turn // 2) % 2) + (core + turn % 2) % 2

    def hop(dim, sign):
        n, at = dims[dim], where[dim]
        if n == 2:
            return b + (1 - 2 * at) * strides[dim], []
        return b + sign * strides[dim], [at < n - 1 if sign > 0 else at > 0]

    def remote(src, dst, send_sem, recv_sem, obs, par):
        return pltpu.make_async_remote_copy(
            src_ref=src, dst_ref=dst, send_sem=send_sem, recv_sem=recv_sem,
            device_id=(obs, par), device_id_type=MESH,
        )

    def here(step):
        conds = []
        for dim, off in enumerate(step[0]):
            if dims[dim] > 2 and off:
                conds.append(where[dim] + off < dims[dim] if off > 0 else where[dim] + off >= 0)
        return conds

    def slot_of(step):
        origin = b
        for dim, off in enumerate(step[0]):
            if off:
                origin = origin + ((1 - 2 * where[dim]) if dims[dim] == 2 else off) * strides[dim]
        source = obs_of(step[1])
        return 4 * origin + source, source

    def is_own(step):
        return step[1] == 0 and not any(step[0])

    def view(step, slot):
        if is_own(step):
            return scaled.at[:, pl.ds(pl.multiple_of(a * quarter, 128), quarter)]
        return panel.at[slot]

    def col_view(step, slot):
        if is_own(step):
            return scaled.at[:, pl.ds(pl.multiple_of(b * width, 128), width)]
        return panel.at[slot, :, pl.ds(pl.multiple_of((b % per) * width, 128), width)]

    def par_copy(step, slot, dim, sign):
        return remote(
            view(step, slot), panel.at[slot], par_send.at[2 * dim + (sign > 0)], recv.at[slot],
            a, hop(dim, sign)[0],
        )

    def col_copies(step, slot, source):
        src = col_view(step, slot)
        return (
            remote(src, cols.at[slot], col_send.at[0], col_recv.at[slot], 2 * chip + 1 - core, b),
            remote(src, cols.at[slot], col_send.at[1], col_recv.at[slot], 2 * (1 - chip) + source % 2, b),
        )

    def relay(slot):
        return remote(
            cols.at[slot], cols.at[slot], col_send.at[2], col_recv.at[slot], 2 * chip + 1 - core, b
        )

    def drain(ref, sem):
        pltpu.make_async_copy(ref, ref, sem).wait()

    def arrive(step):
        def run():
            slot, source = slot_of(step)
            if not is_own(step):
                drain(panel.at[slot], recv.at[slot])
            for dim, sign in forwards(dims, late_first, step):
                guarded(hop(dim, sign)[1], lambda: par_copy(step, slot, dim, sign).start())

            @pl.when(is_owner)
            def _():
                for copy in col_copies(step, slot, source):
                    copy.start()

        guarded(here(step), run)

    def take_cols(step):
        def run():
            slot, source = slot_of(step)
            drain(cols.at[slot], col_recv.at[slot])
            pl.when(jnp.logical_and(jnp.logical_not(on_owner_chip), core == source % 2))(
                lambda: relay(slot).start()
            )

        guarded([jnp.logical_not(is_owner), *here(step)], run)

    def finish():
        long = [dim for dim in range(rank) if dims[dim] > 2]
        for place in itertools.product(*(range(dims[dim]) for dim in long)):
            sent = sends_at(dims, late_first, dict(zip(long, place)))

            def run():
                for way in sorted(sent):
                    drain(panel.at[pl.ds(0, sent[way])], par_send.at[way])

            guarded([where[dim] == at for dim, at in zip(long, place)], run)

        @pl.when(is_owner)
        def _():
            drain(cols, col_send.at[0])
            drain(cols, col_send.at[1])

        pl.when(jnp.logical_not(on_owner_chip))(
            lambda: drain(cols.at[pl.ds(0, cols.shape[0] // 2)], col_send.at[2])
        )

    barrier = pltpu.get_barrier_semaphore()
    mates = [(obs_of(turn), b, []) for turn in (1, 2, 3)]
    for dim in range(rank):
        for sign in (1,) if dims[dim] == 2 else (1, -1):
            mates.append((a, *hop(dim, sign)))
    for obs, par, conds in mates:
        guarded(conds, lambda: pl.semaphore_signal(barrier, inc=1, device_id=(obs, par), device_id_type=MESH))
    count = sum(not conds for _, _, conds in mates)
    for _, _, conds in mates:
        for cond in conds:
            count = count + cond.astype(jnp.int32)
    pl.semaphore_wait(barrier, count)

    mine = 4 * b + a
    to_obs = []
    for turn in (2, 3, 1):
        obs = obs_of(turn)
        to_obs.append(remote(
            scaled.at[:, pl.ds(pl.multiple_of(obs * quarter, 128), quarter)], panel.at[mine],
            obs_send.at[turn], recv.at[mine], obs, b,
        ))
        to_obs[-1].start()
    keep = pltpu.make_async_copy(
        scaled.at[:, pl.ds(pl.multiple_of(a * quarter, 128), quarter)], panel.at[mine], own_sem.at[0]
    )
    keep.start()
    steps = schedule(dims, late_first)
    lag = LAG if rank < 3 else len(steps)
    for i, step in enumerate(steps):
        arrive(step)
        if i >= lag:
            take_cols(steps[i - lag])
    for step in steps[-lag:]:
        take_cols(step)
    keep.wait()
    for copy in to_obs:
        copy.wait_send()
    finish()


def product_kernel(per, panel, panel_all, cols, out, right, sem):
    a, b = lax.axis_index("obs"), lax.axis_index("par")
    width = right.shape[1]

    @pl.when(pl.program_id(0) == 0)
    def _():
        own = pl.ds(pl.multiple_of((b % per) * width, 128), width)

        @pl.when(a == b // per)
        def _():
            pltpu.make_async_copy(panel_all.at[:, own], right, sem).start()

        @pl.when(a != b // per)
        def _():
            pltpu.make_async_copy(cols, right, sem).start()

        pltpu.make_async_copy(cols, right, sem).wait()

    out[...] = lax.dot_general(
        panel[...], right[...], (((0,), (0,)), ((), ())), preferred_element_type=jnp.float32
    )


def on_device(obs_count, par_count, jacobian, obs_weights, time_to_obs):
    rows_here, param_count = jacobian.shape
    indices = jnp.arange(obs_weights.shape[0], dtype=jnp.int32)
    picked = jnp.sum(
        jnp.where(time_to_obs[:, None] == indices[None, :], obs_weights[None, :], 0.0), axis=1
    )
    scaled = (jnp.sqrt(picked)[:, None] * jacobian.astype(jnp.float32)).astype(jnp.bfloat16)
    dims = grid_of(par_count)
    slots = obs_count * par_count
    quarter, width = param_count // obs_count, param_count // par_count
    dma = pltpu.SemaphoreType.DMA
    panel, cols = pl.pallas_call(
        functools.partial(gather_kernel, dims, dims == (4, 2)),
        out_shape=(
            jax.ShapeDtypeStruct((slots, rows_here, quarter), jnp.bfloat16),
            jax.ShapeDtypeStruct((slots, rows_here, width), jnp.bfloat16),
        ),
        in_specs=[pl.BlockSpec(memory_space=pl.ANY)],
        out_specs=(pl.BlockSpec(memory_space=pl.ANY),) * 2,
        scratch_shapes=[
            dma((1,)), dma((slots,)), dma((slots,)), dma((4,)), dma((2 * len(dims),)), dma((3,)),
        ],
        compiler_params=pltpu.CompilerParams(collective_id=0, has_side_effects=True),
        name="gather",
    )(scaled)
    rows = slots * rows_here
    panel, cols = panel.reshape(rows, quarter), cols.reshape(rows, width)
    tile = 512
    return pl.pallas_call(
        functools.partial(product_kernel, quarter // width),
        out_shape=jax.ShapeDtypeStruct((quarter, width), jnp.float32),
        grid=(quarter // tile,),
        in_specs=[
            pl.BlockSpec((rows, tile), lambda i: (0, i)),
            pl.BlockSpec(memory_space=pl.ANY),
            pl.BlockSpec(memory_space=pl.ANY),
        ],
        out_specs=pl.BlockSpec((tile, width), lambda i: (i, 0)),
        scratch_shapes=[pltpu.VMEM((rows, width), jnp.bfloat16), dma],
        compiler_params=pltpu.CompilerParams(vmem_limit_bytes=60 * 2**20, fuse_transposed_lhs_in_matmul=True),
        name="product",
    )(panel, panel, cols)


def solution(mesh):
    placed = (P(("obs", "par"), None), P(), P(("obs", "par")))
    return jax.shard_map(
        functools.partial(on_device, mesh.shape["obs"], mesh.shape["par"]),
        mesh=mesh, in_specs=placed, out_specs=P("obs", "par"), check_vma=False,
    )
```
